1024 devices in a mesh: node: 64 (over z, x), local: 8 (over y), rep: 2 (over core).
Axes of the slice: x: 8, y: 8, z: 8, core: 2. Of those that a mesh axis runs over, the one named last changes fastest.
Arguments:
- act: bfloat16 [32768, 8192], P('node'), may hold values from -16 to 16
- codes: bfloat16 [8192, 2048], P('node', ('local', 'rep')), may hold values from -1 to 1
- scales: float32 [64, 2048], P('node', ('local', 'rep')), may hold values from 0.006629126 to 0.06629126
- cotangent: bfloat16 [32768, 2048], P('node', ('local', 'rep')), may hold values from -0.032958984 to 0.032958984
Outputs:
- keyvals: bfloat16 [32768, 2048], P('node', ('local', 'rep'))
- grad_weight: float32 [8192, 2048], P('node', ('local', 'rep'))
The draws below stay inside these ranges and needn't reach their ends.
All inputs are finite; a program needn't handle non-finite values.
Results may differ from the reference program's by a relative error of at most 0.0049.
Values may be sent and summed in bfloat16 or wider, within the bound.
No kernel may reach another device: no remote copies, remote signals or barrier semaphores. Data moves between devices by JAX's collectives and lax.ppermute only.
A program may use at most 32 MiB of HBM per device.

```python
import math
import jax
import jax.numpy as jnp
from jax import lax

D = 8192
KVW = 2048
QBLOCK = 128
TOKENS = 32768


def with_spikes(array, own_key, source, target, blocks, factor):
    def block_of(position):
        return (jnp.arange(array.shape[position]) // (array.shape[position] // blocks)).reshape((-1,) + (1,) * (array.ndim - 1 - position))

    first = jax.random.permutation(own_key, blocks)[block_of(target)]
    other_side = (block_of(target) + blocks // 2) % blocks
    return jnp.where((block_of(source) == first) | (block_of(source) == other_side), factor * array, array)


def block_scale(own_key, shape, split, least, largest):
    def one(position, parts):
        heights = jax.random.uniform(jax.random.fold_in(jax.random.fold_in(own_key, 6), position), (parts,), jnp.float32, least / len(split), largest / len(split))
        return jnp.repeat(jnp.exp(heights), shape[position] // parts).reshape((-1,) + (1,) * (len(shape) - position - 1))

    gain = one(*split[0])
    for cut in split[1:]:
        gain = gain * one(*cut)
    return gain


def bell_draw(stream_key, dims, scale, bound, cuts=(), kind=jnp.bfloat16):
    drawn = scale * jax.random.normal(stream_key, dims, jnp.float32)
    if cuts:
        drawn = drawn * block_scale(stream_key, dims, cuts, -0.22, 0.18)
    return jnp.clip(drawn, -bound, bound).astype(kind)


def gaussian_with(rng, shape, scale, bound, split, heavy, kind=jnp.bfloat16):
    array = scale * jax.random.normal(rng, shape, jnp.float32)
    if split:
        array = array * block_scale(rng, shape, split, -0.22, 0.18)
    return jnp.clip(with_spikes(array, jax.random.fold_in(rng, 3), *heavy), -bound, bound).astype(kind)


def setup_inputs(seed: int = 0) -> dict:
    streams_of = jax.random.split(jax.random.key(seed), 5)
    act = gaussian_with(streams_of[0], (TOKENS, D), 1.0, 16.0, ((0, 64),), (0, 1, 64, 4.0))
    codes = jnp.clip(jax.random.uniform(streams_of[1], (D, KVW), jnp.float32, -1.0, 1.0) * block_scale(streams_of[1], (D, KVW), ((0, 64), (1, 16)), -0.4, 0.0), -1.0, 1.0).astype(jnp.bfloat16)
    scales = jnp.clip(jnp.exp(math.log(0.06629126) - 2.30258504 * jax.random.uniform(streams_of[2], (D // QBLOCK, KVW), jnp.float32) ** block_scale(streams_of[2], (D // QBLOCK, KVW), ((0, 64), (1, 16)), -0.2, 0.2)), 0.006629126, 0.06629126)
    cotangent = bell_draw(streams_of[3], (TOKENS, KVW), (TOKENS ** -0.5), 0.032958984, ((0, 64), (1, 16)))
    return dict(act=act, codes=codes, scales=scales, cotangent=cotangent)


def reference(act, codes, scales, cotangent):
    full_scales = jnp.repeat(scales, QBLOCK, axis=0)
    weight = (codes.astype(jnp.float32) * full_scales).astype(jnp.bfloat16)
    keyvals = jnp.dot(act, weight, preferred_element_type=jnp.float32).astype(jnp.bfloat16)
    grad_weight = lax.dot_general(act, cotangent, (((0,), (0,)), ((), ())), preferred_element_type=jnp.float32)
    return keyvals, grad_weight
```

```python
import jax
import jax.numpy as jnp
from jax import lax
from jax.sharding import PartitionSpec as P


def body(act, codes, scales, cotangent):
    rows = codes.shape[0]
    per_block = rows // scales.shape[0]
    weight = (codes.astype(jnp.float32) * jnp.repeat(scales, per_block, axis=0)).astype(
        jnp.bfloat16
    )
    gathered = lax.all_gather(weight, "node", axis=0, tiled=True)
    partial = lax.dot_general(
        act, cotangent, (((0,), (0,)), ((), ())), preferred_element_type=jnp.float32
    ).astype(jnp.bfloat16)
    shares = lax.all_to_all(
        partial.reshape(-1, rows, partial.shape[1]), "node", 0, 0, tiled=True
    )
    grad_weight = jnp.sum(shares.astype(jnp.float32), axis=0)
    product = jnp.dot(act, gathered, preferred_element_type=jnp.float32)
    return (product.astype(jnp.bfloat16), grad_weight)


def solution(mesh):
    in_specs = (
        P("node", None),
        P("node", ("local", "rep")),
        P("node", ("local", "rep")),
        P("node", ("local", "rep")),
    )
    out_specs = (P("node", ("local", "rep")), P("node", ("local", "rep")))
    return jax.shard_map(body, mesh=mesh, in_specs=in_specs, out_specs=out_specs, check_vma=False)
```

```python
import functools

import jax
import jax.numpy as jnp
from jax import lax
from jax.experimental import pallas as pl
from jax.experimental.pallas import tpu as pltpu
from jax.sharding import Mesh, PartitionSpec as P

SIDE = 8
AXES = ("z", "x", "rep")


def lines(first):
    at = lambda z, x, r: (z * SIDE + x) * 2 + r
    along_x = [[at(z, x, first) for x in range(SIDE)] for z in range(SIDE)]
    along_z = [[at(z, x, 1 - first) for z in range(SIDE)] for x in range(SIDE)]
    return along_x + along_z


def params():
    return pltpu.CompilerParams(
        dimension_semantics=("arbitrary",), vmem_limit_bytes=32 * 1024 * 1024
    )


def grad_kernel(rep, act, cot, codes, scales, out):
    step = pl.program_id(0)
    rows = codes.shape[0]

    @pl.when(step == 0)
    def _():
        weight = (codes[...].astype(jnp.float32) * scales[...]).astype(jnp.bfloat16)
        for peer in range(SIDE):
            out[peer, SIDE] = weight

    share = lax.dot_general(
        cot[...], act[...], (((0,), (0,)), ((), ())), preferred_element_type=jnp.float32
    ).astype(jnp.bfloat16)
    x_first = rep[0] == 0
    for j in range(SIDE):
        out[jnp.where(x_first, j, step), jnp.where(x_first, step, j)] = share[
            :, j * rows : (j + 1) * rows
        ]


def middle_kernel(shares, weights, out):
    total = shares[0, 0].astype(jnp.float32)
    for peer in range(1, SIDE):
        total += shares[peer, 0].astype(jnp.float32)
    out[0, SIDE] = total.astype(jnp.bfloat16)
    for peer in range(SIDE):
        out[0, peer] = weights[peer, 0]


def keyvals_kernel(rep, act, blocks, out, grad, weight, total):
    step = pl.program_id(0)
    rows = blocks.shape[2]
    x_first = rep[0] == 0
    for j in range(SIDE):
        weight[j * rows : (j + 1) * rows] = blocks[
            jnp.where(x_first, step, j), jnp.where(x_first, j, step)
        ]
    product = jnp.dot(act[...], weight[...], preferred_element_type=jnp.float32)

    @pl.when(step == 0)
    def _():
        total[...] = product
        share = blocks[0, SIDE].astype(jnp.float32)
        for peer in range(1, SIDE):
            share += blocks[peer, SIDE].astype(jnp.float32)
        grad[...] = share.T

    @pl.when(step > 0)
    def _():
        total[...] += product

    @pl.when(step == SIDE - 1)
    def _():
        out[...] = total[...].astype(jnp.bfloat16)


def body(act, codes, scales, cotangent):
    tokens, width = act.shape
    rows, columns = codes.shape
    chunk = width // SIDE
    rep = lax.axis_index("rep").astype(jnp.int32).reshape(1)
    packed = (SIDE, SIDE + 1, columns, rows)
    whole = lambda shape: pl.BlockSpec(shape, lambda i, r: (0,) * len(shape))
    act_spec = pl.BlockSpec((tokens, chunk), lambda i, r: (0, i))
    flops = 2 * tokens * width * columns
    cost = pl.CostEstimate(flops=flops, bytes_accessed=2 * act.size, transcendentals=0)

    sent = pl.pallas_call(
        grad_kernel,
        out_shape=jax.ShapeDtypeStruct(packed, jnp.bfloat16),
        grid_spec=pltpu.PrefetchScalarGridSpec(
            num_scalar_prefetch=1,
            grid=(SIDE,),
            in_specs=[act_spec, whole(cotangent.shape), whole(codes.shape), whole(scales.shape)],
            out_specs=whole(packed),
        ),
        compiler_params=params(),
        cost_estimate=cost,
    )(rep, act, cotangent, codes, scales)

    arrived = lax.all_to_all(sent, AXES, 0, 0, axis_index_groups=lines(0))

    sent = pl.pallas_call(
        middle_kernel,
        out_shape=jax.ShapeDtypeStruct(packed, jnp.bfloat16),
        grid=(SIDE,),
        in_specs=[
            pl.BlockSpec((SIDE, 1, columns, rows), lambda i: (0, i, 0, 0)),
            pl.BlockSpec((SIDE, 1, columns, rows), lambda i: (0, SIDE, 0, 0)),
        ],
        out_specs=pl.BlockSpec((1, SIDE + 1, columns, rows), lambda i: (i, 0, 0, 0)),
        compiler_params=params(),
    )(arrived, arrived)

    arrived = lax.all_to_all(sent, AXES, 0, 0, axis_index_groups=lines(1))

    return tuple(
        pl.pallas_call(
            keyvals_kernel,
            out_shape=(
                jax.ShapeDtypeStruct((tokens, columns), jnp.bfloat16),
                jax.ShapeDtypeStruct((rows, columns), jnp.float32),
            ),
            grid_spec=pltpu.PrefetchScalarGridSpec(
                num_scalar_prefetch=1,
                grid=(SIDE,),
                in_specs=[act_spec, whole(packed)],
                out_specs=(whole((tokens, columns)), whole((rows, columns))),
                scratch_shapes=[
                    pltpu.VMEM((chunk, columns), jnp.bfloat16),
                    pltpu.VMEM((tokens, columns), jnp.float32),
                ],
            ),
            compiler_params=params(),
            cost_estimate=cost,
        )(rep, act, arrived)
    )


def solution(mesh):
    split = Mesh(mesh.devices.reshape(SIDE, SIDE, 8, 2), ("z", "x", "local", "rep"))
    rows, columns = ("z", "x"), ("local", "rep")
    in_specs = (P(rows, None), P(rows, columns), P(rows, columns), P(rows, columns))
    out_specs = (P(rows, columns), P(rows, columns))
    return jax.shard_map(body, mesh=split, in_specs=in_specs, out_specs=out_specs, check_vma=False)
```

```python
import functools

import jax
import jax.numpy as jnp
from jax import lax
from jax.experimental import pallas as pl
from jax.experimental.pallas import tpu as pltpu
from jax.sharding import Mesh, PartitionSpec as P

SIDE = 8
AXES = ("z", "x", "rep")


def lines(first):
    at = lambda z, x, r: (z * SIDE + x) * 2 + r
    along_x = [[at(z, x, first) for x in range(SIDE)] for z in range(SIDE)]
    along_z = [[at(z, x, 1 - first) for z in range(SIDE)] for x in range(SIDE)]
    return along_x + along_z


def params(mib=32):
    return pltpu.CompilerParams(vmem_limit_bytes=mib * 1024 * 1024)


def spot(first, outer, inner):
    return jnp.where(first, inner, outer), jnp.where(first, outer, inner)


def grad_kernel(act, cot, codes, scales, out, act_v, cot_v, codes_v, scales_v, sems):
    rows = codes.shape[0]
    chunk = act.shape[1] // SIDE
    part = lambda k: pl.ds(k * chunk, chunk)
    copies = [
        pltpu.make_async_copy(cot, cot_v, sems.at[0]),
        pltpu.make_async_copy(codes, codes_v, sems.at[1]),
        pltpu.make_async_copy(scales, scales_v, sems.at[2]),
    ] + [
        pltpu.make_async_copy(act.at[:, part(k)], act_v.at[k], sems.at[3 + k]) for k in range(SIDE)
    ]
    for copy in copies:
        copy.start()
    x_first = lax.axis_index("rep") == 0
    copies[1].wait()
    copies[2].wait()
    weight = (codes_v[...].astype(jnp.float32) * scales_v[...]).astype(jnp.bfloat16)
    for peer in range(SIDE):
        out[peer, SIDE] = weight
    copies[0].wait()
    cot_t = cot_v[...].T
    for k in range(SIDE):
        copies[3 + k].wait()
        share = jnp.dot(cot_t, act_v[k], preferred_element_type=jnp.float32).astype(jnp.bfloat16)
        for j in range(SIDE):
            out[spot(x_first, k, j)] = share[:, j * rows : (j + 1) * rows]


def middle_kernel(blocks, out):
    for peer in range(SIDE):
        total = blocks[0, peer].astype(jnp.float32)
        for source in range(1, SIDE):
            total += blocks[source, peer].astype(jnp.float32)
        out[peer, SIDE] = total.astype(jnp.bfloat16)
        for source in range(SIDE):
            out[peer, source] = blocks[source, SIDE]


def keyvals_kernel(act, blocks, out, grad, weight):
    rows = blocks.shape[2]
    chunk = SIDE * rows
    z_last = lax.axis_index("rep") == 1
    total = None
    for k in range(SIDE):
        for j in range(SIDE):
            weight[pl.ds((k * SIDE + j) * rows, rows)] = blocks[spot(z_last, k, j)]
        part = pl.ds(k * chunk, chunk)
        product = jnp.dot(act[:, part], weight[part], preferred_element_type=jnp.float32)
        total = product if total is None else total + product
    out[...] = total.astype(jnp.bfloat16)
    share = blocks[0, SIDE].astype(jnp.float32)
    for peer in range(1, SIDE):
        share += blocks[peer, SIDE].astype(jnp.float32)
    grad[...] = share.T


def body(act, codes, scales, cotangent):
    tokens, width = act.shape
    rows, columns = codes.shape
    packed = (SIDE, SIDE + 1, columns, rows)
    vmem, hbm = pl.BlockSpec(memory_space=pltpu.VMEM), pl.BlockSpec(memory_space=pltpu.HBM)
    flops = 2 * tokens * width * columns
    cost = pl.CostEstimate(flops=flops, bytes_accessed=2 * act.size, transcendentals=0)
    exchange = lambda blocks, groups: lax.all_to_all(blocks, AXES, 0, 0, axis_index_groups=groups)

    sent = pl.pallas_call(
        grad_kernel,
        out_shape=jax.ShapeDtypeStruct(packed, jnp.bfloat16),
        in_specs=[hbm] * 4,
        out_specs=vmem,
        scratch_shapes=[
            pltpu.VMEM((SIDE, tokens, width // SIDE), act.dtype),
            pltpu.VMEM(cotangent.shape, cotangent.dtype),
            pltpu.VMEM(codes.shape, codes.dtype),
            pltpu.VMEM(scales.shape, scales.dtype),
            pltpu.SemaphoreType.DMA((3 + SIDE,)),
        ],
        compiler_params=params(60),
        cost_estimate=cost,
    )(act, cotangent, codes, scales)
    arrived = exchange(sent, lines(0))
    sent = pl.pallas_call(
        middle_kernel,
        out_shape=jax.ShapeDtypeStruct(packed, jnp.bfloat16),
        in_specs=[vmem],
        out_specs=vmem,
        compiler_params=params(),
    )(arrived)
    arrived = exchange(sent, lines(1))
    return tuple(
        pl.pallas_call(
            keyvals_kernel,
            out_shape=(
                jax.ShapeDtypeStruct((tokens, columns), jnp.bfloat16),
                jax.ShapeDtypeStruct((rows, columns), jnp.float32),
            ),
            in_specs=[vmem, vmem],
            out_specs=(vmem, vmem),
            scratch_shapes=[pltpu.VMEM((width, columns), jnp.bfloat16)],
            compiler_params=params(),
            cost_estimate=cost,
        )(act, arrived)
    )


def solution(mesh):
    split = Mesh(mesh.devices.reshape(SIDE, SIDE, 8, 2), ("z", "x", "local", "rep"))
    rows, columns = ("z", "x"), ("local", "rep")
    in_specs = (P(rows, None), P(rows, columns), P(rows, columns), P(rows, columns))
    out_specs = (P(rows, columns), P(rows, columns))
    return jax.shard_map(body, mesh=split, in_specs=in_specs, out_specs=out_specs, check_vma=False)
```

```python
import functools

import jax
import jax.numpy as jnp
from jax import lax
from jax.experimental import pallas as pl
from jax.experimental.pallas import tpu as pltpu
from jax.sharding import Mesh, PartitionSpec as P

SIDE = 8
TIED = 6
AXES = ("z", "x", "rep")


def lines(first):
    at = lambda z, x, r: (z * SIDE + x) * 2 + r
    along_x = [[at(z, x, first) for x in range(SIDE)] for z in range(SIDE)]
    along_z = [[at(z, x, 1 - first) for z in range(SIDE)] for x in range(SIDE)]
    return along_x + along_z


def steps(first, away):
    return [(line[i], line[(i + away) % SIDE]) for line in lines(first) for i in range(SIDE)]


def params(mib=32):
    return pltpu.CompilerParams(vmem_limit_bytes=mib * 1024 * 1024)


def spot(first, outer, inner):
    return jnp.where(first, inner, outer), jnp.where(first, outer, inner)


def weight_kernel(codes, scales, out):
    weight = (codes[...].astype(jnp.float32) * scales[...]).astype(jnp.bfloat16)
    for peer in range(SIDE):
        out[peer] = weight


def grad_kernel(act, cot, out, act_v, cot_v, sems):
    rows = out.shape[3]
    chunk = SIDE * rows
    copies = [pltpu.make_async_copy(cot, cot_v, sems.at[SIDE])] + [
        pltpu.make_async_copy(act.at[:, pl.ds(k * chunk, chunk)], act_v.at[k], sems.at[k])
        for k in range(SIDE)
    ]
    for copy in copies:
        copy.start()
    x_first = lax.axis_index("rep") == 0
    copies[0].wait()
    cot_t = cot_v[...].T
    for k in range(SIDE):
        copies[1 + k].wait()
        share = jnp.dot(cot_t, act_v[k], preferred_element_type=jnp.float32).astype(jnp.bfloat16)
        for j in range(SIDE):
            out[spot(x_first, k, j)] = share[:, j * rows : (j + 1) * rows]


def sum_of(blocks, *rest):
    total = blocks[(0, *rest)].astype(jnp.float32)
    for source in range(1, SIDE):
        total += blocks[(source, *rest)].astype(jnp.float32)
    return total


def middle_kernel(blocks, out):
    for peer in range(SIDE):
        out[peer] = sum_of(blocks, peer).astype(jnp.bfloat16)


def last_kernel(blocks, out):
    out[...] = sum_of(blocks).T


def keyvals_kernel(act, *refs):
    lines_of, (out, act_v, weight, sems) = refs[:SIDE], refs[SIDE:]
    rows = lines_of[0].shape[1]
    chunk = SIDE * rows
    copies = [
        pltpu.make_async_copy(act.at[:, pl.ds(k * chunk, chunk)], act_v.at[k], sems.at[k])
        for k in range(SIDE)
    ]
    for copy in copies:
        copy.start()
    z_last = lax.axis_index("rep") == 0
    me = jnp.where(z_last, lax.axis_index("z"), lax.axis_index("x"))
    for away, line in enumerate(lines_of):
        origin = lax.rem(me + (SIDE - away), SIDE)
        for j in range(SIDE):
            row = jnp.where(z_last, origin * SIDE + j, j * SIDE + origin) * rows
            weight[pl.ds(pl.multiple_of(row, rows), rows)] = line[j]
    total = None
    for k in range(SIDE):
        copies[k].wait()
        product = jnp.dot(
            act_v[k], weight[pl.ds(k * chunk, chunk)], preferred_element_type=jnp.float32
        )
        total = product if total is None else total + product
    out[...] = total.astype(jnp.bfloat16)


def local(kernel, out, args, mib=32, hbm=0, scratch=(), flops=0):
    vmem, far = pl.BlockSpec(memory_space=pltpu.VMEM), pl.BlockSpec(memory_space=pltpu.HBM)
    moved = sum(x.size * x.dtype.itemsize for x in (*args, out))
    return pl.pallas_call(
        kernel,
        out_shape=out,
        in_specs=[far] * hbm + [vmem] * (len(args) - hbm),
        out_specs=vmem,
        scratch_shapes=list(scratch),
        compiler_params=params(mib),
        cost_estimate=pl.CostEstimate(flops=flops, bytes_accessed=moved, transcendentals=0),
    )(*args)


def body(act, codes, scales, cotangent):
    tokens, width = act.shape
    rows, columns = codes.shape
    flops = 2 * tokens * width * columns
    bf16 = lambda *shape: jax.ShapeDtypeStruct(shape, jnp.bfloat16)
    one, all_of = bf16(SIDE, rows, columns), bf16(SIDE, SIDE, columns, rows)
    exchange = lambda blocks, groups: lax.all_to_all(blocks, AXES, 0, 0, axis_index_groups=groups)

    line = exchange(local(weight_kernel, one, (codes, scales)), lines(0))
    shares = local(
        grad_kernel,
        all_of,
        (act, cotangent),
        mib=60,
        hbm=2,
        scratch=(
            pltpu.VMEM((SIDE, tokens, width // SIDE), act.dtype),
            pltpu.VMEM(cotangent.shape, cotangent.dtype),
            pltpu.SemaphoreType.DMA((1 + SIDE,)),
        ),
        flops=flops,
    )
    shares = exchange(shares, lines(0))
    weights = [line] + [lax.ppermute(line, AXES, steps(1, away)) for away in range(1, SIDE)]
    shares, *weights[1:TIED] = lax.optimization_barrier((shares, *weights[1:TIED]))
    shares = exchange(local(middle_kernel, one, (shares,)), lines(1))
    keyvals = local(
        keyvals_kernel,
        bf16(tokens, columns),
        (act, *weights),
        mib=51,
        hbm=1,
        scratch=(
            pltpu.VMEM((SIDE, tokens, width // SIDE), act.dtype),
            pltpu.VMEM((width, columns), jnp.bfloat16),
            pltpu.SemaphoreType.DMA((SIDE,)),
        ),
        flops=flops,
    )
    grad = local(last_kernel, jax.ShapeDtypeStruct((rows, columns), jnp.float32), (shares,))
    return keyvals, grad


def solution(mesh):
    split = Mesh(mesh.devices.reshape(SIDE, SIDE, 8, 2), ("z", "x", "local", "rep"))
    rows, columns = ("z", "x"), ("local", "rep")
    in_specs = (P(rows, None), P(rows, columns), P(rows, columns), P(rows, columns))
    out_specs = (P(rows, columns), P(rows, columns))
    return jax.shard_map(body, mesh=split, in_specs=in_specs, out_specs=out_specs, check_vma=False)
```

```python
import jax
import jax.numpy as jnp
from jax import lax
from jax.experimental import pallas as pl
from jax.experimental.pallas import tpu as pltpu
from jax.sharding import Mesh, PartitionSpec as P

SIDE = 8
HALF = SIDE // 2
AXES = ("z", "x", "rep")


def lines(first):
    at = lambda z, x, r: (z * SIDE + x) * 2 + r
    along_x = [[at(z, x, first) for x in range(SIDE)] for z in range(SIDE)]
    along_z = [[at(z, x, 1 - first) for z in range(SIDE)] for x in range(SIDE)]
    return along_x + along_z


def halves():
    return [line[parity::2] for line in lines(1) for parity in range(2)]


def shift(x, away):
    pairs = [(line[i], line[(i + away) % SIDE]) for line in lines(1) for i in range(SIDE)]
    return lax.ppermute(x, AXES, pairs)


def place():
    along_z = lax.axis_index("rep") == 0
    return along_z, jnp.where(along_z, lax.axis_index("z"), lax.axis_index("x"))


def weight_kernel(codes, scales, out):
    weight = (codes[...].astype(jnp.float32) * scales[...]).astype(jnp.bfloat16)
    for peer in range(SIDE):
        out[peer] = weight


def grad_kernel(act, cot, keep, up, down, act_v, cot_v, out_v, sems):
    rows = keep.shape[3]
    chunk = SIDE * rows
    copies = [pltpu.make_async_copy(cot, cot_v, sems.at[SIDE])] + [
        pltpu.make_async_copy(act.at[:, pl.ds(k * chunk, chunk)], act_v.at[k], sems.at[k])
        for k in range(SIDE)
    ]
    for copy in copies:
        copy.start()
    along_z, me = place()
    copies[0].wait()
    cot_t = cot_v[...].T
    for k in range(SIDE):
        copies[1 + k].wait()
        share = jnp.dot(cot_t, act_v[k], preferred_element_type=jnp.float32).astype(jnp.bfloat16)
        for j in range(SIDE):
            away = lax.rem(jnp.where(along_z, k, j) - me + SIDE, SIDE)
            odd = jnp.where(away < HALF, HALF + away // 2, SIDE + 1 - away // 2)
            slot = jnp.where(lax.rem(away, 2) == 0, away // 2, odd)
            out_v[slot, jnp.where(along_z, j, k)] = share[:, j * rows : (j + 1) * rows]
    back = [
        pltpu.make_async_copy(out_v.at[pl.ds(0, HALF)], keep, sems.at[0]),
        pltpu.make_async_copy(out_v.at[pl.ds(HALF, 2)], up, sems.at[1]),
        pltpu.make_async_copy(out_v.at[pl.ds(HALF + 2, 2)], down, sems.at[2]),
    ]
    for copy in back:
        copy.start()
    for copy in back:
        copy.wait()


def combine_kernel(keep, below, above, line, out):
    me = place()[1] // 2
    wide = lambda block: block.astype(jnp.float32)
    for even in range(HALF):
        peer = lax.rem(me + even, HALF)
        for j in range(SIDE):
            total = wide(keep[even, j])
            if even < 2:
                total += wide(below[even, j])
            if even in (0, HALF - 1):
                total += wide(above[min(even, 1), j])
            out[peer, j] = total.astype(jnp.bfloat16)
        out[even, pl.ds(SIDE, SIDE)] = line[...]


def middle_kernel(blocks, out, up, down):
    me = place()[1] // 2
    for j in range(SIDE):
        total = blocks[0, j].astype(jnp.float32)
        for source in range(1, HALF):
            total += blocks[source, j].astype(jnp.float32)
        out[j] = total.astype(jnp.bfloat16)
    mine = lambda step: blocks[lax.rem(me + step, HALF), pl.ds(SIDE, SIDE)]
    up[0] = down[0] = mine(0)
    up[1] = mine(HALF - 1)
    down[1] = mine(1)


def keyvals_kernel(act, blocks, below, above, out, weight):
    rows = blocks.shape[2]
    chunk = SIDE * rows
    along_z, me = place()

    def put(origin, read):
        for j in range(SIDE):
            row = jnp.where(along_z, origin * SIDE + j, j * SIDE + origin) * rows
            weight[pl.ds(pl.multiple_of(row, rows), rows)] = read(j)

    for half in range(HALF):
        put(lax.rem(me, 2) + 2 * half, lambda j: blocks[half, SIDE + j])
    for k in range(2):
        put(lax.rem(me + 1 + 2 * k, SIDE), lambda j: above[k, j])
        put(lax.rem(me + SIDE - 1 - 2 * k, SIDE), lambda j: below[k, j])
    total = None
    for k in range(SIDE):
        part = pl.ds(k * chunk, chunk)
        product = jnp.dot(act[:, part], weight[part], preferred_element_type=jnp.float32)
        total = product if total is None else total + product
    out[...] = total.astype(jnp.bfloat16)


def last_kernel(blocks, out):
    total = blocks[0].astype(jnp.float32)
    for source in range(1, SIDE):
        total += blocks[source].astype(jnp.float32)
    out[...] = total.T


def local(kernel, out, args, mib=32, far=False, scratch=(), flops=0):
    spec = pl.BlockSpec(memory_space=pltpu.HBM if far else pltpu.VMEM)
    moved = sum(x.size * x.dtype.itemsize for x in (*args, *jax.tree.leaves(out)))
    return pl.pallas_call(
        kernel,
        out_shape=out,
        in_specs=[spec] * len(args),
        out_specs=jax.tree.map(lambda _: spec, out),
        scratch_shapes=list(scratch),
        compiler_params=pltpu.CompilerParams(vmem_limit_bytes=mib * 1024 * 1024),
        cost_estimate=pl.CostEstimate(flops=flops, bytes_accessed=moved, transcendentals=0),
    )(*args)


def body(act, codes, scales, cotangent):
    tokens, width = act.shape
    rows, columns = codes.shape
    flops = 2 * tokens * width * columns
    bf16 = lambda *shape: jax.ShapeDtypeStruct((*shape, columns, rows), jnp.bfloat16)
    one, two = bf16(SIDE), bf16(2, SIDE)
    exchange = lambda blocks, groups: lax.all_to_all(blocks, AXES, 0, 0, axis_index_groups=groups)

    line = exchange(local(weight_kernel, one, (codes, scales)), lines(0))
    keep, up, down = local(
        grad_kernel,
        (bf16(HALF, SIDE), two, two),
        (act, cotangent),
        mib=60,
        far=True,
        scratch=(
            pltpu.VMEM((SIDE, tokens, width // SIDE), act.dtype),
            pltpu.VMEM(cotangent.shape, cotangent.dtype),
            pltpu.VMEM((SIDE, SIDE, columns, rows), jnp.bfloat16),
            pltpu.SemaphoreType.DMA((1 + SIDE,)),
        ),
        flops=flops,
    )
    packed = local(
        combine_kernel, bf16(HALF, 2 * SIDE), (keep, shift(up, 1), shift(down, SIDE - 1), line)
    )
    blocks = exchange(packed, halves())
    shares, up, down = local(middle_kernel, (one, two, two), (blocks,))
    shares = exchange(shares, lines(0))
    keyvals = local(
        keyvals_kernel,
        jax.ShapeDtypeStruct((tokens, columns), jnp.bfloat16),
        (act, blocks, shift(up, 1), shift(down, SIDE - 1)),
        scratch=(pltpu.VMEM((width, columns), jnp.bfloat16),),
        flops=flops,
    )
    grad = local(last_kernel, jax.ShapeDtypeStruct((rows, columns), jnp.float32), (shares,))
    return keyvals, grad


def solution(mesh):
    split = Mesh(mesh.devices.reshape(SIDE, SIDE, 8, 2), ("z", "x", "local", "rep"))
    rows, columns = ("z", "x"), ("local", "rep")
    in_specs = (P(rows, None), P(rows, columns), P(rows, columns), P(rows, columns))
    out_specs = (P(rows, columns), P(rows, columns))
    return jax.shard_map(body, mesh=split, in_specs=in_specs, out_specs=out_specs, check_vma=False)
```

```python
import jax
import jax.numpy as jnp
from jax import lax
from jax.experimental import pallas as pl
from jax.experimental.pallas import tpu as pltpu
from jax.sharding import Mesh, PartitionSpec as P

SIDE = 8
HALF = SIDE // 2
AXES = ("z", "x", "rep")


def lines(first):
    at = lambda z, x, r: (z * SIDE + x) * 2 + r
    along_x = [[at(z, x, first) for x in range(SIDE)] for z in range(SIDE)]
    along_z = [[at(z, x, 1 - first) for z in range(SIDE)] for x in range(SIDE)]
    return along_x + along_z


def halves():
    return [line[parity::2] for line in lines(1) for parity in range(2)]


def shift(x, away):
    pairs = [(line[i], line[(i + away) % SIDE]) for line in lines(1) for i in range(SIDE)]
    return lax.ppermute(x, AXES, pairs)


def place():
    along_z = lax.axis_index("rep") == 0
    return along_z, jnp.where(along_z, lax.axis_index("z"), lax.axis_index("x"))


def weight_kernel(codes, scales, out):
    weight = (codes[...].astype(jnp.float32) * scales[...]).astype(jnp.bfloat16)
    for peer in range(SIDE):
        out[peer] = weight


def grad_kernel(act, cot, keep, up, down, act_v, cot_v, out_v, sems):
    rows = keep.shape[3]
    chunk = SIDE * rows
    copies = [pltpu.make_async_copy(cot, cot_v, sems.at[SIDE])] + [
        pltpu.make_async_copy(act.at[:, pl.ds(k * chunk, chunk)], act_v.at[k], sems.at[k])
        for k in range(SIDE)
    ]
    for copy in copies:
        copy.start()
    along_z, me = place()
    copies[0].wait()
    cot_t = cot_v[...].T
    for k in range(SIDE):
        copies[1 + k].wait()
        share = jnp.dot(cot_t, act_v[k], preferred_element_type=jnp.float32).astype(jnp.bfloat16)
        for j in range(SIDE):
            away = lax.rem(jnp.where(along_z, k, j) - me + SIDE, SIDE)
            odd = jnp.where(away < HALF, HALF + away // 2, SIDE + 1 - away // 2)
            slot = jnp.where(lax.rem(away, 2) == 0, away // 2, odd)
            out_v[slot, jnp.where(along_z, j, k)] = share[:, j * rows : (j + 1) * rows]
    back = [
        pltpu.make_async_copy(out_v.at[pl.ds(0, HALF)], keep, sems.at[0]),
        pltpu.make_async_copy(out_v.at[pl.ds(HALF, 2)], up, sems.at[1]),
        pltpu.make_async_copy(out_v.at[pl.ds(HALF + 2, 2)], down, sems.at[2]),
    ]
    for copy in back:
        copy.start()
    for copy in back:
        copy.wait()


def combine_kernel(keep, below, above, line, out):
    me = place()[1] // 2
    wide = lambda block: block.astype(jnp.float32)
    for even in range(HALF):
        peer = lax.rem(me + even, HALF)
        for j in range(SIDE):
            total = wide(keep[even, j])
            if even < 2:
                total += wide(below[even, j])
            if even in (0, HALF - 1):
                total += wide(above[min(even, 1), j])
            out[peer, j] = total.astype(jnp.bfloat16)
        out[even, pl.ds(SIDE, SIDE)] = line[...]


def middle_kernel(blocks, out, up, down):
    me = place()[1] // 2
    for j in range(SIDE):
        total = blocks[0, j].astype(jnp.float32)
        for source in range(1, HALF):
            total += blocks[source, j].astype(jnp.float32)
        out[j] = total.astype(jnp.bfloat16)
    mine = lambda step: blocks[lax.rem(me + step, HALF), pl.ds(SIDE, SIDE)]
    up[0] = down[0] = mine(0)
    up[1] = mine(HALF - 1)
    down[1] = mine(1)


def keyvals_kernel(act, blocks, below, above, out, weight):
    rows = blocks.shape[2]
    chunk = SIDE * rows
    along_z, me = place()

    def put(origin, read):
        for j in range(SIDE):
            row = jnp.where(along_z, origin * SIDE + j, j * SIDE + origin) * rows
            weight[pl.ds(pl.multiple_of(row, rows), rows)] = read(j)

    for half in range(HALF):
        put(lax.rem(me, 2) + 2 * half, lambda j: blocks[half, SIDE + j])
    for k in range(2):
        put(lax.rem(me + 1 + 2 * k, SIDE), lambda j: above[k, j])
        put(lax.rem(me + SIDE - 1 - 2 * k, SIDE), lambda j: below[k, j])
    total = None
    for k in range(SIDE):
        part = pl.ds(k * chunk, chunk)
        product = jnp.dot(act[:, part], weight[part], preferred_element_type=jnp.float32)
        total = product if total is None else total + product
    out[...] = total.astype(jnp.bfloat16)


def last_kernel(blocks, out):
    total = blocks[0].astype(jnp.float32)
    for source in range(1, SIDE):
        total += blocks[source].astype(jnp.float32)
    out[...] = total.T


def local(kernel, out, args, mib=32, far=False, scratch=(), flops=0):
    spec = pl.BlockSpec(memory_space=pltpu.HBM if far else pltpu.VMEM)
    moved = sum(x.size * x.dtype.itemsize for x in (*args, *jax.tree.leaves(out)))
    return pl.pallas_call(
        kernel,
        out_shape=out,
        in_specs=[spec] * len(args),
        out_specs=jax.tree.map(lambda _: spec, out),
        scratch_shapes=list(scratch),
        compiler_params=pltpu.CompilerParams(vmem_limit_bytes=mib * 1024 * 1024),
        cost_estimate=pl.CostEstimate(flops=flops, bytes_accessed=moved, transcendentals=0),
    )(*args)


def body(act, codes, scales, cotangent):
    tokens, width = act.shape
    rows, columns = codes.shape
    flops = 2 * tokens * width * columns
    bf16 = lambda *shape: jax.ShapeDtypeStruct((*shape, columns, rows), jnp.bfloat16)
    one, two = bf16(SIDE), bf16(2, SIDE)
    exchange = lambda blocks, groups: lax.all_to_all(blocks, AXES, 0, 0, axis_index_groups=groups)

    line = exchange(local(weight_kernel, one, (codes, scales)), lines(0))
    keep, up, down = local(
        grad_kernel,
        (bf16(HALF, SIDE), two, two),
        (act, cotangent),
        mib=60,
        far=True,
        scratch=(
            pltpu.VMEM((SIDE, tokens, width // SIDE), act.dtype),
            pltpu.VMEM(cotangent.shape, cotangent.dtype),
            pltpu.VMEM((SIDE, SIDE, columns, rows), jnp.bfloat16),
            pltpu.SemaphoreType.DMA((1 + SIDE,)),
        ),
        flops=flops,
    )
    line, down = lax.optimization_barrier((line, down))
    packed = local(
        combine_kernel, bf16(HALF, 2 * SIDE), (keep, shift(up, 1), shift(down, SIDE - 1), line)
    )
    blocks = exchange(packed, halves())
    shares, up, down = local(middle_kernel, (one, two, two), (blocks,))
    shares = exchange(shares, lines(0))
    keyvals = local(
        keyvals_kernel,
        jax.ShapeDtypeStruct((tokens, columns), jnp.bfloat16),
        (act, blocks, shift(up, 1), shift(down, SIDE - 1)),
        scratch=(pltpu.VMEM((width, columns), jnp.bfloat16),),
        flops=flops,
    )
    shares, keyvals = lax.optimization_barrier((shares, keyvals))
    grad = local(last_kernel, jax.ShapeDtypeStruct((rows, columns), jnp.float32), (shares,))
    return keyvals, grad


def solution(mesh):
    split = Mesh(mesh.devices.reshape(SIDE, SIDE, 8, 2), ("z", "x", "local", "rep"))
    rows, columns = ("z", "x"), ("local", "rep")
    in_specs = (P(rows, None), P(rows, columns), P(rows, columns), P(rows, columns))
    out_specs = (P(rows, columns), P(rows, columns))
    return jax.shard_map(body, mesh=split, in_specs=in_specs, out_specs=out_specs, check_vma=False)
```

```python
import jax
import jax.numpy as jnp
from jax import lax
from jax.experimental import pallas as pl
from jax.experimental.pallas import tpu as pltpu
from jax.sharding import Mesh, PartitionSpec as P

SIDE = 8
AXES = ("z", "x", "rep")


def lines(first):
    at = lambda z, x, r: (z * SIDE + x) * 2 + r
    along_x = [[at(z, x, first) for x in range(SIDE)] for z in range(SIDE)]
    along_z = [[at(z, x, 1 - first) for z in range(SIDE)] for x in range(SIDE)]
    return along_x + along_z


def params(mib=32):
    return pltpu.CompilerParams(vmem_limit_bytes=mib * 1024 * 1024)


def grad_kernel(
    act, cot, codes, scales, out, act_v, cot_v, codes_v, scales_v, out_v, weight_v, sems, out_sems
):
    rows = codes.shape[0]
    chunk = act.shape[1] // SIDE
    part = lambda k: pl.ds(k * chunk, chunk)
    blocks = pl.ds(0, SIDE)
    copies = [
        pltpu.make_async_copy(codes, codes_v, sems.at[1]),
        pltpu.make_async_copy(scales, scales_v, sems.at[2]),
        pltpu.make_async_copy(cot, cot_v, sems.at[0]),
    ] + [
        pltpu.make_async_copy(act.at[:, part(k)], act_v.at[k], sems.at[3 + k]) for k in range(SIDE)
    ]
    for copy in copies:
        copy.start()
    x_first = lax.axis_index("rep") == 0
    copies[0].wait()
    copies[1].wait()
    weight_v[...] = (codes_v[...].astype(jnp.float32) * scales_v[...]).astype(jnp.bfloat16)
    sent = [
        pltpu.make_async_copy(weight_v, out.at[peer, SIDE], out_sems.at[SIDE + peer])
        for peer in range(SIDE)
    ]
    for copy in sent:
        copy.start()
    copies[2].wait()
    cot_t = cot_v[...].T
    for k in range(SIDE):
        copies[3 + k].wait()
        share = jnp.dot(cot_t, act_v[k], preferred_element_type=jnp.float32).astype(jnp.bfloat16)
        for j in range(SIDE):
            out_v[k, j] = share[:, j * rows : (j + 1) * rows]
        across = pltpu.make_async_copy(out_v.at[k], out.at[blocks, k], out_sems.at[k])
        along = pltpu.make_async_copy(out_v.at[k], out.at[k, blocks], out_sems.at[k])
        pl.when(x_first)(across.start)
        pl.when(jnp.logical_not(x_first))(along.start)
        sent.append(along)
    for copy in sent:
        copy.wait()


def middle_kernel(blocks, out):
    for peer in range(SIDE):
        total = blocks[0, peer].astype(jnp.float32)
        for source in range(1, SIDE):
            total += blocks[source, peer].astype(jnp.float32)
        out[peer, SIDE] = total.astype(jnp.bfloat16)
        for source in range(SIDE):
            out[peer, source] = blocks[source, SIDE]


def keyvals_kernel(act, blocks, out, grad, weight):
    rows = blocks.shape[2]
    chunk = SIDE * rows
    part = lambda k: pl.ds(k * chunk, chunk)
    z_last = lax.axis_index("rep") == 0

    def multiply(weight_of):
        total = None
        for k in range(SIDE):
            product = jnp.dot(act[:, part(k)], weight_of(k), preferred_element_type=jnp.float32)
            total = product if total is None else total + product
        out[...] = total.astype(jnp.bfloat16)

    @pl.when(z_last)
    def _():
        multiply(lambda k: blocks[k, pl.ds(0, SIDE)].reshape(chunk, -1))

    @pl.when(jnp.logical_not(z_last))
    def _():
        for k in range(SIDE):
            for j in range(SIDE):
                weight[pl.ds((k * SIDE + j) * rows, rows)] = blocks[j, k]
        multiply(lambda k: weight[part(k)])

    share = blocks[0, SIDE].astype(jnp.float32)
    for peer in range(1, SIDE):
        share += blocks[peer, SIDE].astype(jnp.float32)
    grad[...] = share.T


def body(act, codes, scales, cotangent):
    tokens, width = act.shape
    rows, columns = codes.shape
    packed = (SIDE, SIDE + 1, columns, rows)
    vmem, hbm = pl.BlockSpec(memory_space=pltpu.VMEM), pl.BlockSpec(memory_space=pltpu.HBM)
    flops = 2 * tokens * width * columns
    cost = pl.CostEstimate(flops=flops, bytes_accessed=2 * act.size, transcendentals=0)
    exchange = lambda blocks, groups: lax.all_to_all(blocks, AXES, 0, 0, axis_index_groups=groups)

    sent = pl.pallas_call(
        grad_kernel,
        out_shape=jax.ShapeDtypeStruct(packed, jnp.bfloat16),
        in_specs=[hbm] * 4,
        out_specs=hbm,
        scratch_shapes=[
            pltpu.VMEM((SIDE, tokens, width // SIDE), act.dtype),
            pltpu.VMEM(cotangent.shape, cotangent.dtype),
            pltpu.VMEM(codes.shape, codes.dtype),
            pltpu.VMEM(scales.shape, scales.dtype),
            pltpu.VMEM((SIDE, SIDE, columns, rows), jnp.bfloat16),
            pltpu.VMEM((rows, columns), jnp.bfloat16),
            pltpu.SemaphoreType.DMA((3 + SIDE,)),
            pltpu.SemaphoreType.DMA((2 * SIDE,)),
        ],
        compiler_params=params(60),
        cost_estimate=cost,
    )(act, cotangent, codes, scales)
    arrived = exchange(sent, lines(0))
    sent = pl.pallas_call(
        middle_kernel,
        out_shape=jax.ShapeDtypeStruct(packed, jnp.bfloat16),
        in_specs=[vmem],
        out_specs=vmem,
        compiler_params=params(),
    )(arrived)
    arrived = exchange(sent, lines(1))
    return tuple(
        pl.pallas_call(
            keyvals_kernel,
            out_shape=(
                jax.ShapeDtypeStruct((tokens, columns), jnp.bfloat16),
                jax.ShapeDtypeStruct((rows, columns), jnp.float32),
            ),
            in_specs=[vmem, vmem],
            out_specs=(vmem, vmem),
            scratch_shapes=[pltpu.VMEM((width, columns), jnp.bfloat16)],
            compiler_params=params(),
            cost_estimate=cost,
        )(act, arrived)
    )


def solution(mesh):
    split = Mesh(mesh.devices.reshape(SIDE, SIDE, 8, 2), ("z", "x", "local", "rep"))
    rows, columns = ("z", "x"), ("local", "rep")
    in_specs = (P(rows, None), P(rows, columns), P(rows, columns), P(rows, columns))
    out_specs = (P(rows, columns), P(rows, columns))
    return jax.shard_map(body, mesh=split, in_specs=in_specs, out_specs=out_specs, check_vma=False)
```

```python
import jax
import jax.numpy as jnp
from jax import lax
from jax.experimental import pallas as pl
from jax.experimental.pallas import tpu as pltpu
from jax.sharding import Mesh, PartitionSpec as P

SIDE = 8
AXES = ("z", "x", "rep")


def listed(place):
    return 3 * place % SIDE


def lines(first):
    at = lambda z, x, r: (z * SIDE + x) * 2 + r
    along_x = [[at(z, listed(x), first) for x in range(SIDE)] for z in range(SIDE)]
    along_z = [[at(listed(z), x, 1 - first) for z in range(SIDE)] for x in range(SIDE)]
    return along_x + along_z


def params(mib=32):
    return pltpu.CompilerParams(vmem_limit_bytes=mib * 1024 * 1024)


def spot(first, outer, inner):
    return jnp.where(first, inner, outer), jnp.where(first, outer, inner)


def grad_kernel(act, cot, codes, scales, out, act_v, cot_v, codes_v, scales_v, sems):
    rows = codes.shape[0]
    chunk = act.shape[1] // SIDE
    part = lambda k: pl.ds(k * chunk, chunk)
    copies = [
        pltpu.make_async_copy(cot, cot_v, sems.at[0]),
        pltpu.make_async_copy(codes, codes_v, sems.at[1]),
        pltpu.make_async_copy(scales, scales_v, sems.at[2]),
    ] + [
        pltpu.make_async_copy(act.at[:, part(k)], act_v.at[k], sems.at[3 + k]) for k in range(SIDE)
    ]
    for copy in copies:
        copy.start()
    x_first = lax.axis_index("rep") == 0
    copies[1].wait()
    copies[2].wait()
    weight = (codes_v[...].astype(jnp.float32) * scales_v[...]).astype(jnp.bfloat16)
    for peer in range(SIDE):
        out[peer, SIDE] = weight
    copies[0].wait()
    cot_t = cot_v[...].T
    for k in range(SIDE):
        copies[3 + k].wait()
        share = jnp.dot(cot_t, act_v[k], preferred_element_type=jnp.float32).astype(jnp.bfloat16)
        for j in range(SIDE):
            out[spot(x_first, listed(k), listed(j))] = share[:, j * rows : (j + 1) * rows]


def middle_kernel(blocks, out):
    for peer in range(SIDE):
        total = blocks[0, peer].astype(jnp.float32)
        for source in range(1, SIDE):
            total += blocks[source, peer].astype(jnp.float32)
        out[peer, SIDE] = total.astype(jnp.bfloat16)
        for source in range(SIDE):
            out[peer, source] = blocks[source, SIDE]


def keyvals_kernel(act, blocks, out, grad, weight):
    rows = blocks.shape[2]
    chunk = SIDE * rows
    z_last = lax.axis_index("rep") == 1
    total = None
    for k in range(SIDE):
        for j in range(SIDE):
            weight[pl.ds((k * SIDE + j) * rows, rows)] = blocks[spot(z_last, listed(k), listed(j))]
        part = pl.ds(k * chunk, chunk)
        product = jnp.dot(act[:, part], weight[part], preferred_element_type=jnp.float32)
        total = product if total is None else total + product
    out[...] = total.astype(jnp.bfloat16)
    share = blocks[0, SIDE].astype(jnp.float32)
    for peer in range(1, SIDE):
        share += blocks[peer, SIDE].astype(jnp.float32)
    grad[...] = share.T


def body(act, codes, scales, cotangent):
    tokens, width = act.shape
    rows, columns = codes.shape
    packed = (SIDE, SIDE + 1, columns, rows)
    vmem, hbm = pl.BlockSpec(memory_space=pltpu.VMEM), pl.BlockSpec(memory_space=pltpu.HBM)
    flops = 2 * tokens * width * columns
    cost = pl.CostEstimate(flops=flops, bytes_accessed=2 * act.size, transcendentals=0)
    exchange = lambda blocks, groups: lax.all_to_all(blocks, AXES, 0, 0, axis_index_groups=groups)

    sent = pl.pallas_call(
        grad_kernel,
        out_shape=jax.ShapeDtypeStruct(packed, jnp.bfloat16),
        in_specs=[hbm] * 4,
        out_specs=vmem,
        scratch_shapes=[
            pltpu.VMEM((SIDE, tokens, width // SIDE), act.dtype),
            pltpu.VMEM(cotangent.shape, cotangent.dtype),
            pltpu.VMEM(codes.shape, codes.dtype),
            pltpu.VMEM(scales.shape, scales.dtype),
            pltpu.SemaphoreType.DMA((3 + SIDE,)),
        ],
        compiler_params=params(60),
        cost_estimate=cost,
    )(act, cotangent, codes, scales)
    arrived = exchange(sent, lines(0))
    sent = pl.pallas_call(
        middle_kernel,
        out_shape=jax.ShapeDtypeStruct(packed, jnp.bfloat16),
        in_specs=[vmem],
        out_specs=vmem,
        compiler_params=params(),
    )(arrived)
    arrived = exchange(sent, lines(1))
    return tuple(
        pl.pallas_call(
            keyvals_kernel,
            out_shape=(
                jax.ShapeDtypeStruct((tokens, columns), jnp.bfloat16),
                jax.ShapeDtypeStruct((rows, columns), jnp.float32),
            ),
            in_specs=[vmem, vmem],
            out_specs=(vmem, vmem),
            scratch_shapes=[pltpu.VMEM((width, columns), jnp.bfloat16)],
            compiler_params=params(),
            cost_estimate=cost,
        )(act, arrived)
    )


def solution(mesh):
    split = Mesh(mesh.devices.reshape(SIDE, SIDE, 8, 2), ("z", "x", "local", "rep"))
    rows, columns = ("z", "x"), ("local", "rep")
    in_specs = (P(rows, None), P(rows, columns), P(rows, columns), P(rows, columns))
    out_specs = (P(rows, columns), P(rows, columns))
    return jax.shard_map(body, mesh=split, in_specs=in_specs, out_specs=out_specs, check_vma=False)
```

```python
import jax
import jax.numpy as jnp
from jax import lax
from jax.experimental import pallas as pl
from jax.experimental.pallas import tpu as pltpu
from jax.sharding import Mesh, PartitionSpec as P

SIDE = 8
AXES = ("z", "x", "rep")


def listed(place):
    return 3 * place % SIDE


def lines(first, order):
    at = lambda z, x, r: (z * SIDE + x) * 2 + r
    along_x = [[at(z, order(x), first) for x in range(SIDE)] for z in range(SIDE)]
    along_z = [[at(order(z), x, 1 - first) for z in range(SIDE)] for x in range(SIDE)]
    return along_x + along_z


def params(mib=32):
    return pltpu.CompilerParams(vmem_limit_bytes=mib * 1024 * 1024)


def grad_kernel(act, cot, codes, scales, out, act_v, cot_v, codes_v, scales_v, sems):
    rows = codes.shape[0]
    chunk = act.shape[1] // SIDE
    part = lambda k: pl.ds(k * chunk, chunk)
    copies = [
        pltpu.make_async_copy(cot, cot_v, sems.at[0]),
        pltpu.make_async_copy(codes, codes_v, sems.at[1]),
        pltpu.make_async_copy(scales, scales_v, sems.at[2]),
    ] + [
        pltpu.make_async_copy(act.at[:, part(k)], act_v.at[k], sems.at[3 + k]) for k in range(SIDE)
    ]
    for copy in copies:
        copy.start()
    x_first = lax.axis_index("rep") == 0
    copies[1].wait()
    copies[2].wait()
    weight = (codes_v[...].astype(jnp.float32) * scales_v[...]).astype(jnp.bfloat16)
    for peer in range(SIDE):
        out[peer, SIDE] = weight
    copies[0].wait()
    cot_t = cot_v[...].T
    for k in range(SIDE):
        copies[3 + k].wait()
        share = jnp.dot(cot_t, act_v[k], preferred_element_type=jnp.float32).astype(jnp.bfloat16)
        for j in range(SIDE):
            peer, rest = jnp.where(x_first, listed(j), listed(k)), jnp.where(x_first, k, j)
            out[peer, rest] = share[:, j * rows : (j + 1) * rows]


def middle_kernel(blocks, out):
    for peer in range(SIDE):
        total = blocks[0, peer].astype(jnp.float32)
        for source in range(1, SIDE):
            total += blocks[source, peer].astype(jnp.float32)
        out[peer, SIDE] = total.astype(jnp.bfloat16)
        for source in range(SIDE):
            out[peer, source] = blocks[source, SIDE]


def keyvals_kernel(act, blocks, out, grad, weight):
    rows = blocks.shape[2]
    chunk = SIDE * rows
    z_last = lax.axis_index("rep") == 1
    total = None
    for k in range(SIDE):
        for j in range(SIDE):
            peer, rest = jnp.where(z_last, j, k), jnp.where(z_last, listed(k), listed(j))
            weight[pl.ds((k * SIDE + j) * rows, rows)] = blocks[peer, rest]
        part = pl.ds(k * chunk, chunk)
        product = jnp.dot(act[:, part], weight[part], preferred_element_type=jnp.float32)
        total = product if total is None else total + product
    out[...] = total.astype(jnp.bfloat16)
    share = blocks[0, SIDE].astype(jnp.float32)
    for peer in range(1, SIDE):
        share += blocks[peer, SIDE].astype(jnp.float32)
    grad[...] = share.T


def body(act, codes, scales, cotangent):
    tokens, width = act.shape
    rows, columns = codes.shape
    packed = (SIDE, SIDE + 1, columns, rows)
    vmem, hbm = pl.BlockSpec(memory_space=pltpu.VMEM), pl.BlockSpec(memory_space=pltpu.HBM)
    flops = 2 * tokens * width * columns
    cost = pl.CostEstimate(flops=flops, bytes_accessed=2 * act.size, transcendentals=0)
    exchange = lambda blocks, groups: lax.all_to_all(blocks, AXES, 0, 0, axis_index_groups=groups)

    sent = pl.pallas_call(
        grad_kernel,
        out_shape=jax.ShapeDtypeStruct(packed, jnp.bfloat16),
        in_specs=[hbm] * 4,
        out_specs=vmem,
        scratch_shapes=[
            pltpu.VMEM((SIDE, tokens, width // SIDE), act.dtype),
            pltpu.VMEM(cotangent.shape, cotangent.dtype),
            pltpu.VMEM(codes.shape, codes.dtype),
            pltpu.VMEM(scales.shape, scales.dtype),
            pltpu.SemaphoreType.DMA((3 + SIDE,)),
        ],
        compiler_params=params(60),
        cost_estimate=cost,
    )(act, cotangent, codes, scales)
    arrived = exchange(sent, lines(0, listed))
    sent = pl.pallas_call(
        middle_kernel,
        out_shape=jax.ShapeDtypeStruct(packed, jnp.bfloat16),
        in_specs=[vmem],
        out_specs=vmem,
        compiler_params=params(),
    )(arrived)
    arrived = exchange(sent, lines(1, int))
    return tuple(
        pl.pallas_call(
            keyvals_kernel,
            out_shape=(
                jax.ShapeDtypeStruct((tokens, columns), jnp.bfloat16),
                jax.ShapeDtypeStruct((rows, columns), jnp.float32),
            ),
            in_specs=[vmem, vmem],
            out_specs=(vmem, vmem),
            scratch_shapes=[pltpu.VMEM((width, columns), jnp.bfloat16)],
            compiler_params=params(),
            cost_estimate=cost,
        )(act, arrived)
    )


def solution(mesh):
    split = Mesh(mesh.devices.reshape(SIDE, SIDE, 8, 2), ("z", "x", "local", "rep"))
    rows, columns = ("z", "x"), ("local", "rep")
    in_specs = (P(rows, None), P(rows, columns), P(rows, columns), P(rows, columns))
    out_specs = (P(rows, columns), P(rows, columns))
    return jax.shard_map(body, mesh=split, in_specs=in_specs, out_specs=out_specs, check_vma=False)
```
